1024 devices in a mesh: tile: 128 (over y, x, z_hi), tracer: 8 (over z_lo, core).
Axes of the slice: x: 4, y: 8, z: 16 (z_hi: 4, z_lo: 4; z = z_hi * 4 + z_lo), core: 2. Of those that a mesh axis runs over, the one named last changes fastest.
Arguments:
- tracers: float32 [96, 8, 1024, 128], P('tracer', None, 'tile'), may hold values from 0.2 to 5
- courant_x: float32 [8, 1024, 128], P('tracer', 'tile'), may hold values from -0.45 to 0.45
- courant_y: float32 [8, 1024, 128], P('tracer', 'tile'), may hold values from -0.45 to 0.45
- kdiff: float32 [8, 1024, 128], P('tracer', 'tile'), may hold values from 0.05 to 4
- humidity: float32 [8, 1024, 128], P('tracer', 'tile'), may hold values from 0 to 0.9
- land: int32 [1024, 128], P('tile'), may hold values 0 or 1
- band_class: int32 [96], replicated, may hold values from 0 to 7
- opt_table: float32 [8, 14], replicated, may hold values from 0.002 to 0.02
- hyg_table: float32 [8], replicated, may hold values from 0.2 to 1
Outputs:
- tracers_out: float32 [96, 8, 1024, 128], P('tracer', None, 'tile')
- extinction: float32 [8, 14, 1024, 128], P('tracer', None, 'tile')
The draws below stay inside these ranges and needn't reach their ends.
Inputs may be any that keep to these rules, and one draw needn't show every extreme that they name: land holds only 0 and 1. band_class indexes rows of opt_table and hyg_table.
All inputs are finite; a program needn't handle non-finite values. No bound on the sum of `land` on one device may be relied on, other than what follows from the above.
Results may differ from the reference program's by a relative error of at most 0.0003.
Values sent between devices are 32-bit elements; how exact they have to be, the bound alone decides.
A program may use at most 32 MiB of HBM per device.

```python
import math
import jax
import jax.numpy as jnp
from jax import lax

TRACERS = 96
BANDS = 14
NCLASS = 8
LEV = 8
NY = 128
NX = 1024


def plant(array, own_key, least, largest):
    dims = array.shape
    index_at = [jax.random.randint(jax.random.fold_in(own_key, axis), (), 0, dims[axis]) for axis in range(len(dims))]
    array = array.at[tuple(index_at)].set(least)
    longest = dims.index(max(dims))
    index_at[longest] = (index_at[longest] + 1) % dims[longest]
    return array.at[tuple(index_at)].set(largest)


def block_scale(rng, dims, split, low, top_value):
    level = 1.0
    for position, shards_of in split:
        draws = jax.random.uniform(jax.random.fold_in(jax.random.fold_in(rng, 6), position), (shards_of,), jnp.float32, low / len(split), top_value / len(split))
        level = level * jnp.repeat(jnp.exp(draws), dims[position] // shards_of).reshape((-1,) + (1,) * (len(dims) - 1 - position))
    return level


def setup_inputs(seed: int = 0) -> dict:
    splits = jax.random.split(jax.random.key(seed), 10)
    tracers = jnp.clip(jnp.exp(math.log(5.0) - 3.218876 * jax.random.uniform(splits[0], (TRACERS, LEV, NX, NY), jnp.float32) ** block_scale(splits[0], (TRACERS, LEV, NX, NY), ((0, 8), (2, 128)), -0.2, 0.2)), 0.2, 5.0)
    courant_x = jnp.clip(jax.random.uniform(splits[1], (LEV, NX, NY), jnp.float32, -0.45, 0.45) * block_scale(splits[1], (LEV, NX, NY), ((0, 8), (1, 128)), -0.4, 0.0), -0.45, 0.45)
    courant_y = jnp.clip(jax.random.uniform(splits[2], (LEV, NX, NY), jnp.float32, -0.45, 0.45) * block_scale(splits[2], (LEV, NX, NY), ((0, 8), (1, 128)), -0.4, 0.0), -0.45, 0.45)
    kdiff = jnp.clip(jnp.exp(math.log(4.0) - 4.3820266 * jax.random.uniform(splits[3], (LEV, NX, NY), jnp.float32) ** block_scale(splits[3], (LEV, NX, NY), ((0, 8), (1, 128)), -0.2, 0.2)), 0.05, 4.0)
    humidity = jnp.clip(0.9 * jax.random.uniform(splits[4], (LEV, NX, NY), jnp.float32) ** block_scale(splits[4], (LEV, NX, NY), ((0, 8), (1, 128)), -0.2, 0.2), 0.0, 0.9)
    land = plant((jax.random.randint(splits[5], (NX, NY), 0, 3) < 1).astype(jnp.int32), jax.random.fold_in(splits[5], 1), 0, 1)
    band_class = plant(jax.random.randint(splits[6], (TRACERS,), 0, NCLASS), jax.random.fold_in(splits[6], 1), 0, NCLASS - 1).astype(jnp.int32)
    opt_table = jnp.clip(jnp.exp(jax.random.uniform(splits[7], (NCLASS, BANDS), jnp.float32, math.log(0.002), math.log(0.02))), 0.002, 0.02)
    hyg_table = jnp.clip(jax.random.uniform(splits[8], (NCLASS,), jnp.float32, 0.2, 1.0), 0.2, 1.0)
    return dict(tracers=tracers, courant_x=courant_x, courant_y=courant_y, kdiff=kdiff, humidity=humidity, land=land, band_class=band_class, opt_table=opt_table, hyg_table=hyg_table)


def minmod(left_step, right_step):
    return 0.5 * (jnp.sign(left_step) + jnp.sign(right_step)) * jnp.minimum(jnp.abs(left_step), jnp.abs(right_step))


def flux_divergence(values, courant, along):
    behind = jnp.roll(values, 1, along)
    leading = jnp.roll(values, -1, along)
    slopes = minmod(values - behind, leading - values)
    face_value = jnp.where(courant >= 0, behind + 0.5 * (1.0 - courant) * jnp.roll(slopes, 1, along), values - 0.5 * (1.0 + courant) * slopes)
    fluxes = courant * face_value
    return jnp.roll(fluxes, -1, along) - fluxes


def column_solve(values, coupling):
    levels_total = coupling.shape[0]
    upper_coef = []
    forward = []
    previous_upper = None
    previous_solved = None
    for height in range(levels_total):
        lower_link = coupling[height]
        source = values[..., height, :, :]
        if height == 0:
            divisor = 1.0 + lower_link
            solved = source / divisor
        else:
            upper_link = coupling[height - 1]
            divisor = 1.0 + upper_link + lower_link + upper_link * previous_upper
            solved = (source + upper_link * previous_solved) / divisor
        previous_upper = -lower_link / divisor
        previous_solved = solved
        upper_coef.append(previous_upper)
        forward.append(solved)
    result = [forward[-1]] * levels_total
    current = forward[-1]
    for height in range(levels_total - 2, -1, -1):
        current = forward[height] - upper_coef[height] * current
        result[height] = current
    return jnp.stack(result, axis=-3)


def reference(tracers, courant_x, courant_y, kdiff, humidity, land, band_class, opt_table, hyg_table):
    surface = kdiff[-1:] * (0.25 + 0.75 * land.astype(jnp.float32))[None]
    coupling = jnp.concatenate([kdiff[:-1], surface], 0)
    dryness = jnp.log(1.0 - humidity)

    def advance(values):
        moved = values - flux_divergence(values, courant_x, 1) - flux_divergence(values, courant_y, 2)
        return column_solve(moved, coupling)

    def one_tracer(summed, inputs):
        values, class_id = inputs
        final = advance(advance(values))
        swelling = jnp.exp(-hyg_table[class_id] * dryness)
        summed = summed + (final * swelling)[:, None] * opt_table[class_id][None, :, None, None]
        return summed, final

    extinction, finals = lax.scan(one_tracer, jnp.zeros((LEV, BANDS, NX, NY), jnp.float32), (tracers, band_class))
    return finals, extinction
```

```python
import functools

import jax
import jax.numpy as jnp
from jax import lax
from jax.experimental import pallas as pl
from jax.experimental.pallas import tpu as pltpu
from jax.sharding import PartitionSpec as P

MESH = pl.DeviceIdType.MESH
F32 = jnp.float32
TR = 12
LEV = 8
ROWS = 8
NY = 128
NCLASS = 8
BANDS = 14
GROUP = 8
CHIPS = 4
PER = 3
CHUNKS = TR // PER

X0, XS0, XC, XSC, X1, XS1, GA, GB, HA, HB, YGA, YGB, YHA, YHB, INV, UP, LOW = range(17)
NCOEF = 17


def limited(near, far):
    return jnp.minimum(jnp.maximum(near, jnp.minimum(far, 0.0)), jnp.maximum(far, 0.0))


def roll_rows(a, by):
    return pltpu.roll(a, by % ROWS, 0)


def roll_lanes(a, by):
    return pltpu.roll(a, by % NY, 1)


def face_coefs(c):
    plus, minus = jnp.maximum(c, 0.0), jnp.minimum(c, 0.0)
    return plus, plus * (0.5 * (1.0 - c)), minus, minus * (-0.5 * (1.0 + c))


def kernel(
    tiles,
    x_hbm, cx_hbm, cy_hbm, kd_hbm, hum_hbm, land_hbm, cls_ref, opt_ref, hyg_ref,
    out_ref, ext_ref,
    ext, fields, kd, hum, land, coef, sbuf, spair, sx, sr, swell,
    ready, loc, own, hs, hr, es, er, gs, gr, ps, pr, xs, xr,
):
    me, k = lax.axis_index("tile"), lax.axis_index("tracer")
    right, left = lax.rem(me + 1, tiles), lax.rem(me + tiles - 1, tiles)
    chip, core = k // 2, lax.rem(k, 2)

    loads = [
        pltpu.make_async_copy(cx_hbm, fields.at[pl.ds(k, 1), 0, pl.ds(4, ROWS)], loc.at[0]),
        pltpu.make_async_copy(cy_hbm, fields.at[pl.ds(k, 1), 1, pl.ds(4, ROWS)], loc.at[1]),
        pltpu.make_async_copy(kd_hbm, kd, loc.at[2]),
        pltpu.make_async_copy(hum_hbm, hum, loc.at[3]),
        pltpu.make_async_copy(land_hbm, land, loc.at[4]),
    ]
    for copy in loads:
        copy.start()

    barrier = pltpu.get_barrier_semaphore()
    pl.semaphore_signal(barrier, inc=1, device_id=(left, k), device_id_type=MESH)
    for step in range(1, GROUP):
        pl.semaphore_signal(
            barrier, inc=1, device_id=(me, lax.rem(k + step, GROUP)), device_id_type=MESH
        )
    own_copy = pltpu.make_async_copy(x_hbm, ext.at[:, :, pl.ds(4, ROWS), :], own)
    own_copy.start()
    pl.semaphore_wait(barrier, GROUP)
    pl.semaphore_signal(ready, inc=1, device_id=(right, k), device_id_type=MESH)

    def halo(half, chunk):
        t = pl.ds(chunk * PER, PER)
        return pltpu.make_async_remote_copy(
            src_ref=x_hbm.at[t, :, pl.ds(4 - 4 * half, 4), :],
            dst_ref=ext.at[t, :, pl.ds(12 * half, 4), :],
            send_sem=hs.at[half, chunk],
            recv_sem=hr.at[half, chunk],
            device_id=((left if half else right), k),
            device_id_type=MESH,
        )

    def edge(half):
        src, dst, count = ((10, 2, 2), (4, 12, 4))[half]
        return pltpu.make_async_remote_copy(
            src_ref=fields.at[k, :, pl.ds(src, count), :],
            dst_ref=fields.at[k, :, pl.ds(dst, count), :],
            send_sem=es.at[half],
            recv_sem=er.at[half],
            device_id=((left if half else right), k),
            device_id_type=MESH,
        )

    def spread(part, step):
        first, count = ((2, 2), (12, 4), (4, ROWS))[part]
        return pltpu.make_async_remote_copy(
            src_ref=fields.at[k, :, pl.ds(first, count), :],
            dst_ref=fields.at[k, :, pl.ds(first, count), :],
            send_sem=gs.at[part, step],
            recv_sem=gr.at[part, k],
            device_id=(me, lax.rem(k + step, GROUP)),
            device_id_type=MESH,
        )

    def spread_wait(part, step):
        first, count = ((2, 2), (12, 4), (4, ROWS))[part]
        other = lax.rem(k + step, GROUP)
        pltpu.make_async_remote_copy(
            src_ref=fields.at[other, :, pl.ds(first, count), :],
            dst_ref=fields.at[other, :, pl.ds(first, count), :],
            send_sem=gs.at[part, step],
            recv_sem=gr.at[part, other],
            device_id=(me, other),
            device_id_type=MESH,
        ).wait_recv()

    halo(0, 0).start()
    for copy in loads:
        copy.wait()
    lowest = jnp.where(k == LEV - 1, 1.0, 0.0).astype(F32)
    fields[k, 2, pl.ds(4, ROWS), :] = kd[0] * (
        1.0 + lowest * (0.25 + 0.75 * land[...].astype(F32) - 1.0)
    )
    edge(0).start()
    for step in range(1, GROUP):
        spread(2, step).start()
    for chunk in range(1, CHUNKS):
        halo(0, chunk).start()

    dryness = jnp.log(1.0 - hum[0])
    for c in range(NCLASS):
        swell[c] = jnp.exp(-hyg_ref[c] * dryness)

    pl.semaphore_wait(ready, 1)
    edge(1).start()
    for chunk in range(CHUNKS):
        halo(1, chunk).start()

    for half in (1, 0):
        edge(half).wait_recv()
        for step in range(1, GROUP):
            spread(half, step).start()
    for part in (2, 1, 0):
        for step in range(1, GROUP):
            spread_wait(part, step)

    def coefficients(half):
        base = 4 * half
        upper = previous = None
        for level in range(LEV):
            p0, r0, q0, t0 = face_coefs(fields[level, 0, pl.ds(base + 2, ROWS), :])
            p1, r1, q1, t1 = face_coefs(fields[level, 0, pl.ds(base + 3, ROWS), :])
            put = lambda row, value: coef.__setitem__((half, level, row), value)
            put(X0, p0)
            put(XS0, r0)
            put(XC, 1.0 + q0 - p1)
            put(XSC, t0 - r1)
            put(X1, -q1)
            put(XS1, -t1)
            put(GA, p1)
            put(GB, r1)
            put(HA, q0)
            put(HB, t0)
            yp, yr, yq, yt = face_coefs(fields[level, 1, pl.ds(base + 2, ROWS), :])
            put(YGA, roll_lanes(yp, -1))
            put(YGB, roll_lanes(yr, -1))
            put(YHA, yq)
            put(YHB, yt)
            lower = fields[level, 2, pl.ds(base + 2, ROWS), :]
            if level == 0:
                inverse = 1.0 / (1.0 + lower)
                put(UP, jnp.zeros_like(inverse))
            else:
                inverse = 1.0 / (1.0 + upper + lower - upper * previous)
                put(UP, upper * inverse)
            previous = lower * inverse
            upper = lower
            put(INV, inverse)
            put(LOW, previous)

    coefficients(1)
    coefficients(0)
    own_copy.wait()

    def mixed(moved, half):
        forward = []
        for level in range(LEV):
            solved = moved[level] * coef[half, level, INV]
            if level:
                solved = solved + coef[half, level, UP] * forward[-1]
            forward.append(solved)
        for level in range(LEV - 2, -1, -1):
            forward[level] = forward[level] + coef[half, level, LOW] * forward[level + 1]
        return forward

    def along_y(v, half, level):
        jump = v - roll_lanes(v, 1)
        slope = limited(jump, roll_lanes(jump, -1))
        ahead = coef[half, level, YGA] * v + coef[half, level, YGB] * slope
        flux = roll_lanes(ahead, 1) + coef[half, level, YHA] * v + coef[half, level, YHB] * slope
        return flux - roll_lanes(flux, -1)

    def two_steps(t, half):
        base = 4 * half
        moved = []
        for level in range(LEV):
            v = [ext[t, level, pl.ds(base + n, ROWS), :] for n in range(5)]
            jump = [v[n + 1] - v[n] for n in range(4)]
            slope = [limited(jump[n], jump[n + 1]) for n in range(3)]
            c = lambda row: coef[half, level, row]
            moved.append(
                (c(X0) * v[1] + c(XS0) * slope[0])
                + (c(XC) * v[2] + c(XSC) * slope[1])
                + (c(X1) * v[3] + c(XS1) * slope[2])
                + along_y(v[2], half, level)
            )
        middle = mixed(moved, half)
        moved = []
        for level in range(LEV):
            m = middle[level]
            c = lambda row: coef[half, level, row]
            jump = m - roll_rows(m, 1)
            slope = limited(jump, roll_rows(jump, -1))
            flux = roll_rows(c(GA) * m + c(GB) * slope, 1) + c(HA) * m + c(HB) * slope
            moved.append(m + flux - roll_rows(flux, -1) + along_y(m, half, level))
        final = mixed(moved, half)
        for level in range(LEV):
            out_ref[t, level, pl.ds(base, 4), :] = final[level][2:6, :]

    def do_chunk(half, chunk):
        halo(half ^ 0, chunk).wait_recv()
        first = chunk * PER

        def body(i, carry):
            two_steps(first + i, half)
            return carry

        lax.fori_loop(0, PER, body, 0)
        rows = pl.ds(4 * half, 4)
        weights = []
        for i in range(PER):
            own_class = cls_ref[k * TR + first + i]
            weights.append([jnp.where(own_class == c, 1.0, 0.0).astype(F32) for c in range(NCLASS)])
        for level in range(LEV):
            values = [out_ref[first + i, level, rows, :] for i in range(PER)]
            at = (level % 2, level // 2)
            for c in range(NCLASS):
                total = sum(weights[i][c] * values[i] for i in range(PER))
                if chunk:
                    total = total + sbuf[at[0], at[1], c, rows, :]
                sbuf[at[0], at[1], c, rows, :] = total

    def pair(half, step):
        to = lax.rem(chip + step, CHIPS)
        rows = pl.ds(4 * half, 4)
        return pltpu.make_async_remote_copy(
            src_ref=sbuf.at[1 - core, to, :, rows, :],
            dst_ref=spair.at[to, :, rows, :],
            send_sem=ps.at[half, step],
            recv_sem=pr.at[half, step],
            device_id=(me, 2 * chip + 1 - core),
            device_id_type=MESH,
        )

    def cross(half, step):
        to = lax.rem(chip + step, CHIPS)
        rows = pl.ds(4 * half, 4)
        return pltpu.make_async_remote_copy(
            src_ref=sx.at[to, :, rows, :],
            dst_ref=sr.at[step, :, rows, :],
            send_sem=xs.at[half, step],
            recv_sem=xr.at[half, step],
            device_id=(me, 2 * to + core),
            device_id_type=MESH,
        )

    def start_pair(half):
        for step in (2, 1, 3, 0):
            pair(half, step).start()

    def start_cross(half):
        rows = pl.ds(4 * half, 4)
        for step in (2, 1, 3, 0):
            pair(half, step).wait_recv()
            to = lax.rem(chip + step, CHIPS)
            sx[to, :, rows, :] = sbuf[core, to, :, rows, :] + spair[to, :, rows, :]
            if step:
                cross(half, step).start()

    for chunk in range(CHUNKS):
        do_chunk(1, chunk)
    start_pair(1)
    for chunk in range(CHUNKS):
        do_chunk(0, chunk)
        if chunk == 0:
            start_cross(1)
    start_pair(0)
    start_cross(0)
    for half in (1, 0):
        for step in range(1, CHIPS):
            cross(half, step).wait_recv()
    wetted = []
    for c in range(NCLASS):
        total = (sx[chip, c] + sr[1, c]) + (sr[2, c] + sr[3, c])
        wetted.append(total * swell[c])
    for b in range(BANDS):
        ext_ref[0, b] = sum(opt_ref[c, b] * wetted[c] for c in range(NCLASS))

    for half in (0, 1):
        edge(half).wait_send()
        for chunk in range(CHUNKS):
            halo(half, chunk).wait_send()
        for step in range(CHIPS):
            pair(half, step).wait_send()
            if step:
                cross(half, step).wait_send()
    for part in range(3):
        for step in range(1, GROUP):
            spread(part, step).wait_send()


def local(tiles, tracers, courant_x, courant_y, kdiff, humidity, land, band_class, opt_table, hyg_table):
    hbm = pl.BlockSpec(memory_space=pltpu.HBM)
    vmem = pl.BlockSpec(memory_space=pltpu.VMEM)
    smem = pl.BlockSpec(memory_space=pltpu.SMEM)
    dma = pltpu.SemaphoreType.DMA
    return tuple(
        pl.pallas_call(
            functools.partial(kernel, tiles),
            out_shape=(
                jax.ShapeDtypeStruct((TR, LEV, ROWS, NY), F32),
                jax.ShapeDtypeStruct((1, BANDS, ROWS, NY), F32),
            ),
            in_specs=[hbm] * 6 + [smem] * 3,
            out_specs=(vmem, vmem),
            scratch_shapes=[
                pltpu.VMEM((TR, LEV, 16, NY), F32),
                pltpu.VMEM((LEV, 3, 16, NY), F32),
                pltpu.VMEM((1, ROWS, NY), F32),
                pltpu.VMEM((1, ROWS, NY), F32),
                pltpu.VMEM((ROWS, NY), jnp.int32),
                pltpu.VMEM((2, LEV, NCOEF, ROWS, NY), F32),
                pltpu.VMEM((2, CHIPS, NCLASS, ROWS, NY), F32),
                pltpu.VMEM((CHIPS, NCLASS, ROWS, NY), F32),
                pltpu.VMEM((CHIPS, NCLASS, ROWS, NY), F32),
                pltpu.VMEM((CHIPS, NCLASS, ROWS, NY), F32),
                pltpu.VMEM((NCLASS, ROWS, NY), F32),
                pltpu.SemaphoreType.REGULAR,
                dma((5,)),
                dma,
                dma((2, CHUNKS)),
                dma((2, CHUNKS)),
                dma((2,)),
                dma((2,)),
                dma((3, GROUP)),
                dma((3, GROUP)),
                dma((2, CHIPS)),
                dma((2, CHIPS)),
                dma((2, CHIPS)),
                dma((2, CHIPS)),
            ],
            compiler_params=pltpu.CompilerParams(
                collective_id=0, has_side_effects=True, vmem_limit_bytes=32 << 20
            ),
        )(tracers, courant_x, courant_y, kdiff, humidity, land, band_class, opt_table, hyg_table)
    )


def solution(mesh):
    in_specs = (
        P("tracer", None, "tile", None),
        P("tracer", "tile", None),
        P("tracer", "tile", None),
        P("tracer", "tile", None),
        P("tracer", "tile", None),
        P("tile", None),
        P(),
        P(),
        P(),
    )
    out_specs = (P("tracer", None, "tile", None), P("tracer", None, "tile", None))
    return jax.shard_map(
        functools.partial(local, mesh.shape["tile"]),
        mesh=mesh, in_specs=in_specs, out_specs=out_specs, check_vma=False,
    )
```

```python
import functools

import jax
import jax.numpy as jnp
from jax import lax
from jax.experimental import pallas as pl
from jax.experimental.pallas import tpu as pltpu
from jax.sharding import PartitionSpec as P

MESH = pl.DeviceIdType.MESH
F32 = jnp.float32
TR = 12
LEV = 8
ROWS = 8
NY = 128
NCLASS = 8
BANDS = 14
GROUP = 8
CHIPS = 4
PER = 3
CHUNKS = TR // PER

V, V2, XJ0, XJ1, XS0, XS1, XS2, GA, GB, HA, HB, YJ0, YJ1, YS0, YS1, YS2, INV, UP, LOW = range(19)
NCOEF = 19
ROWS_CHUNK = PER * LEV * ROWS


def limited(near, far):
    return jnp.minimum(jnp.maximum(near, jnp.minimum(far, 0.0)), jnp.maximum(far, 0.0))


def roll_rows(a, by):
    return pltpu.roll(a, by % ROWS, 0)


def roll_lanes(a, by):
    return pltpu.roll(a, by % NY, 1)


def face_coefs(c):
    plus, minus = jnp.maximum(c, 0.0), jnp.minimum(c, 0.0)
    return plus, plus * (0.5 * (1.0 - c)), minus, minus * (-0.5 * (1.0 + c))


def kernel(
    tiles,
    x_hbm, cx_hbm, cy_hbm, kd_hbm, hum_hbm, land_hbm, cls_ref, opt_ref, hyg_ref,
    out_ref, ext_ref,
    ext, fields, kd, hum, land, coef, shift, jumps, middle_ref, sbuf, spair, sx, sr, swell,
    ready, loc, own, hs, hr, es, er, gs, gr, ps, pr, xs, xr,
):
    me, k = lax.axis_index("tile"), lax.axis_index("tracer")
    right, left = lax.rem(me + 1, tiles), lax.rem(me + tiles - 1, tiles)
    chip, core = k // 2, lax.rem(k, 2)

    loads = [
        pltpu.make_async_copy(cx_hbm, fields.at[pl.ds(k, 1), 0, pl.ds(4, ROWS)], loc.at[0]),
        pltpu.make_async_copy(cy_hbm, fields.at[pl.ds(k, 1), 1, pl.ds(4, ROWS)], loc.at[1]),
        pltpu.make_async_copy(kd_hbm, kd, loc.at[2]),
        pltpu.make_async_copy(hum_hbm, hum, loc.at[3]),
        pltpu.make_async_copy(land_hbm, land, loc.at[4]),
    ]
    for copy in loads:
        copy.start()

    barrier = pltpu.get_barrier_semaphore()
    pl.semaphore_signal(barrier, inc=1, device_id=(left, k), device_id_type=MESH)
    for step in range(1, GROUP):
        pl.semaphore_signal(
            barrier, inc=1, device_id=(me, lax.rem(k + step, GROUP)), device_id_type=MESH
        )
    own_copy = pltpu.make_async_copy(x_hbm, ext.at[:, :, pl.ds(4, ROWS), :], own)
    own_copy.start()
    pl.semaphore_wait(barrier, GROUP)
    pl.semaphore_signal(ready, inc=1, device_id=(right, k), device_id_type=MESH)

    def halo(half, chunk):
        t = pl.ds(chunk * PER, PER)
        return pltpu.make_async_remote_copy(
            src_ref=x_hbm.at[t, :, pl.ds(4 - 4 * half, 4), :],
            dst_ref=ext.at[t, :, pl.ds(12 * half, 4), :],
            send_sem=hs.at[half, chunk],
            recv_sem=hr.at[half, chunk],
            device_id=((left if half else right), k),
            device_id_type=MESH,
        )

    def edge(half):
        src, dst, count = ((10, 2, 2), (4, 12, 4))[half]
        return pltpu.make_async_remote_copy(
            src_ref=fields.at[k, :, pl.ds(src, count), :],
            dst_ref=fields.at[k, :, pl.ds(dst, count), :],
            send_sem=es.at[half],
            recv_sem=er.at[half],
            device_id=((left if half else right), k),
            device_id_type=MESH,
        )

    def spread(part, step):
        first, count = ((2, 2), (12, 4), (4, ROWS))[part]
        return pltpu.make_async_remote_copy(
            src_ref=fields.at[k, :, pl.ds(first, count), :],
            dst_ref=fields.at[k, :, pl.ds(first, count), :],
            send_sem=gs.at[part, step],
            recv_sem=gr.at[part, k],
            device_id=(me, lax.rem(k + step, GROUP)),
            device_id_type=MESH,
        )

    def spread_wait(part, step):
        first, count = ((2, 2), (12, 4), (4, ROWS))[part]
        other = lax.rem(k + step, GROUP)
        pltpu.make_async_remote_copy(
            src_ref=fields.at[other, :, pl.ds(first, count), :],
            dst_ref=fields.at[other, :, pl.ds(first, count), :],
            send_sem=gs.at[part, step],
            recv_sem=gr.at[part, other],
            device_id=(me, other),
            device_id_type=MESH,
        ).wait_recv()

    halo(0, 0).start()
    for copy in loads:
        copy.wait()
    lowest = jnp.where(k == LEV - 1, 1.0, 0.0).astype(F32)
    fields[k, 2, pl.ds(4, ROWS), :] = kd[0] * (
        1.0 + lowest * (0.25 + 0.75 * land[...].astype(F32) - 1.0)
    )
    edge(0).start()
    for step in range(1, GROUP):
        spread(2, step).start()
    for chunk in range(1, CHUNKS):
        halo(0, chunk).start()

    dryness = jnp.log(1.0 - hum[0])
    for c in range(NCLASS):
        swell[c] = jnp.exp(-hyg_ref[c] * dryness)

    pl.semaphore_wait(ready, 1)
    edge(1).start()
    for chunk in range(CHUNKS):
        halo(1, chunk).start()

    for half in (1, 0):
        edge(half).wait_recv()
        for step in range(1, GROUP):
            spread(half, step).start()
    for part in (2, 1, 0):
        for step in range(1, GROUP):
            spread_wait(part, step)

    from_y = lax.broadcasted_iota(jnp.int32, (2 * NY, NY), 0) % NY
    to_y = lax.broadcasted_iota(jnp.int32, (2 * NY, NY), 1)
    for n in range(4):
        plus = jnp.where(from_y == (to_y + n + NY - 1) % NY, 1.0, 0.0)
        minus = jnp.where(from_y == (to_y + n + NY - 2) % NY, 1.0, 0.0)
        shift[:, pl.ds(n * NY, NY)] = (plus - minus).astype(jnp.bfloat16)
    sbuf[...] = jnp.zeros_like(sbuf)

    def coefficients(half):
        base = 4 * half
        upper = previous = None
        for level in range(LEV):
            c0 = fields[level, 0, pl.ds(base + 2, ROWS), :]
            c1 = fields[level, 0, pl.ds(base + 3, ROWS), :]
            p0, r0, q0, t0 = face_coefs(c0)
            p1, r1, q1, t1 = face_coefs(c1)
            put = lambda row, value: coef.__setitem__((half, level, row), value)
            put(XJ0, -p0)
            put(XJ1, -q1)
            put(XS0, r0)
            put(XS1, t0 - r1)
            put(XS2, -t1)
            put(GA, p1)
            put(GB, r1)
            put(HA, q0)
            put(HB, t0)
            d0 = fields[level, 1, pl.ds(base + 2, ROWS), :]
            d1 = roll_lanes(d0, -1)
            put(V, 1.0 + (c0 - c1) + (d0 - d1))
            put(V2, 1.0 + (d0 - d1))
            p0, r0, q0, t0 = face_coefs(d0)
            p1, r1, q1, t1 = face_coefs(d1)
            put(YJ0, -p0)
            put(YJ1, -q1)
            put(YS0, r0)
            put(YS1, t0 - r1)
            put(YS2, -t1)
            lower = fields[level, 2, pl.ds(base + 2, ROWS), :]
            if level == 0:
                inverse = 1.0 / (1.0 + lower)
                put(UP, jnp.zeros_like(inverse))
            else:
                inverse = 1.0 / (1.0 + upper + lower - upper * previous)
                put(UP, upper * inverse)
            previous = lower * inverse
            upper = lower
            put(INV, inverse)
            put(LOW, previous)

    coefficients(1)
    coefficients(0)
    own_copy.wait()

    def mixed(moved, half):
        forward = []
        for level in range(LEV):
            solved = moved[level] * coef[half, level, INV]
            if level:
                solved = solved + coef[half, level, UP] * forward[-1]
            forward.append(solved)
        for level in range(LEV - 2, -1, -1):
            forward[level] = forward[level] + coef[half, level, LOW] * forward[level + 1]
        return forward

    def jumps_along_y(v):
        lead = v.astype(jnp.bfloat16)
        trail = (v - lead.astype(F32)).astype(jnp.bfloat16)
        jumps[...] = jnp.dot(
            jnp.concatenate([lead, trail], 1), shift[...], preferred_element_type=F32
        )

    def along_y(row, c):
        jump = [jumps[pl.ds(row, ROWS), pl.ds(n * NY, NY)] for n in range(4)]
        slope = [limited(jump[n], jump[n + 1]) for n in range(3)]
        return (
            (c(YJ0) * jump[1] + c(YJ1) * jump[2])
            + (c(YS0) * slope[0] + c(YS1) * slope[1])
            + c(YS2) * slope[2]
        )

    def first_step(i, t, half):
        base = 4 * half
        moved = []
        for level in range(LEV):
            c = lambda row: coef[half, level, row]
            v = [ext[t, level, pl.ds(base + n, ROWS), :] for n in range(5)]
            jump = [v[n + 1] - v[n] for n in range(4)]
            slope = [limited(jump[n], jump[n + 1]) for n in range(3)]
            row = pl.multiple_of((i * LEV + level) * ROWS, ROWS)
            moved.append(
                (c(V) * v[2] + c(XJ0) * jump[1])
                + (c(XJ1) * jump[2] + c(XS0) * slope[0])
                + (c(XS1) * slope[1] + c(XS2) * slope[2])
                + along_y(row, c)
            )
        moved = mixed(moved, half)
        for level in range(LEV):
            row = pl.multiple_of((i * LEV + level) * ROWS, ROWS)
            middle_ref[pl.ds(row, ROWS), :] = moved[level]

    def second_step(i, t, half):
        moved = []
        for level in range(LEV):
            c = lambda row: coef[half, level, row]
            row = pl.multiple_of((i * LEV + level) * ROWS, ROWS)
            m = middle_ref[pl.ds(row, ROWS), :]
            jump = m - roll_rows(m, 1)
            slope = limited(jump, roll_rows(jump, -1))
            flux = roll_rows(c(GA) * m + c(GB) * slope, 1) + c(HA) * m + c(HB) * slope
            moved.append((c(V2) * m + flux) - roll_rows(flux, -1) + along_y(row, c))
        final = mixed(moved, half)
        for level in range(LEV):
            out_ref[t, level, pl.ds(4 * half, 4), :] = final[level][2:6, :]

    def do_chunk(half, chunk):
        halo(half, chunk).wait_recv()
        first = chunk * PER
        own_rows = ext[pl.ds(first, PER), :, pl.ds(4 * half + 2, ROWS), :]
        jumps_along_y(own_rows.reshape(ROWS_CHUNK, NY))

        def first_body(i, carry):
            first_step(i, first + i, half)
            return carry

        def second_body(i, carry):
            second_step(i, first + i, half)
            return carry

        lax.fori_loop(0, PER, first_body, 0)
        jumps_along_y(middle_ref[...])
        lax.fori_loop(0, PER, second_body, 0)
        rows = pl.ds(4 * half, 4)
        weights = []
        for i in range(PER):
            own_class = cls_ref[k * TR + first + i]
            weights.append([jnp.where(own_class == c, 1.0, 0.0).astype(F32) for c in range(NCLASS)])
        for level in range(LEV):
            values = [out_ref[first + i, level, rows, :] for i in range(PER)]
            at = (level % 2, level // 2)
            for c in range(NCLASS):
                total = sum(weights[i][c] * values[i] for i in range(PER))
                sbuf[at[0], at[1], c, rows, :] = sbuf[at[0], at[1], c, rows, :] + total

    def pair(half, step):
        to = lax.rem(chip + step, CHIPS)
        rows = pl.ds(4 * half, 4)
        return pltpu.make_async_remote_copy(
            src_ref=sbuf.at[1 - core, to, :, rows, :],
            dst_ref=spair.at[to, :, rows, :],
            send_sem=ps.at[half, step],
            recv_sem=pr.at[half, step],
            device_id=(me, 2 * chip + 1 - core),
            device_id_type=MESH,
        )

    def cross(half, step):
        to = lax.rem(chip + step, CHIPS)
        rows = pl.ds(4 * half, 4)
        return pltpu.make_async_remote_copy(
            src_ref=sx.at[to, :, rows, :],
            dst_ref=sr.at[step, :, rows, :],
            send_sem=xs.at[half, step],
            recv_sem=xr.at[half, step],
            device_id=(me, 2 * to + core),
            device_id_type=MESH,
        )

    def start_pair(half):
        for step in (2, 1, 3, 0):
            pair(half, step).start()

    def start_cross(half):
        rows = pl.ds(4 * half, 4)
        for step in (2, 1, 3, 0):
            pair(half, step).wait_recv()
            to = lax.rem(chip + step, CHIPS)
            sx[to, :, rows, :] = sbuf[core, to, :, rows, :] + spair[to, :, rows, :]
            if step:
                cross(half, step).start()

    def after_body(chunk, carry):
        do_chunk(1, chunk)
        return carry

    def before_body(chunk, carry):
        do_chunk(0, chunk)

        @pl.when(chunk == 0)
        def _():
            start_cross(1)

        return carry

    lax.fori_loop(0, CHUNKS, after_body, 0)
    start_pair(1)
    lax.fori_loop(0, CHUNKS, before_body, 0)
    start_pair(0)
    start_cross(0)
    for half in (1, 0):
        for step in range(1, CHIPS):
            cross(half, step).wait_recv()
    wetted = []
    for c in range(NCLASS):
        total = (sx[chip, c] + sr[1, c]) + (sr[2, c] + sr[3, c])
        wetted.append(total * swell[c])
    for b in range(BANDS):
        ext_ref[0, b] = sum(opt_ref[c, b] * wetted[c] for c in range(NCLASS))

    for half in (0, 1):
        edge(half).wait_send()
        for chunk in range(CHUNKS):
            halo(half, chunk).wait_send()
        for step in range(CHIPS):
            pair(half, step).wait_send()
            if step:
                cross(half, step).wait_send()
    for part in range(3):
        for step in range(1, GROUP):
            spread(part, step).wait_send()


def local(tiles, tracers, courant_x, courant_y, kdiff, humidity, land, band_class, opt_table, hyg_table):
    hbm = pl.BlockSpec(memory_space=pltpu.HBM)
    vmem = pl.BlockSpec(memory_space=pltpu.VMEM)
    smem = pl.BlockSpec(memory_space=pltpu.SMEM)
    dma = pltpu.SemaphoreType.DMA
    return tuple(
        pl.pallas_call(
            functools.partial(kernel, tiles),
            out_shape=(
                jax.ShapeDtypeStruct((TR, LEV, ROWS, NY), F32),
                jax.ShapeDtypeStruct((1, BANDS, ROWS, NY), F32),
            ),
            in_specs=[hbm] * 6 + [smem] * 3,
            out_specs=(vmem, vmem),
            scratch_shapes=[
                pltpu.VMEM((TR, LEV, 16, NY), F32),
                pltpu.VMEM((LEV, 3, 16, NY), F32),
                pltpu.VMEM((1, ROWS, NY), F32),
                pltpu.VMEM((1, ROWS, NY), F32),
                pltpu.VMEM((ROWS, NY), jnp.int32),
                pltpu.VMEM((2, LEV, NCOEF, ROWS, NY), F32),
                pltpu.VMEM((2 * NY, 4 * NY), jnp.bfloat16),
                pltpu.VMEM((ROWS_CHUNK, 4 * NY), F32),
                pltpu.VMEM((ROWS_CHUNK, NY), F32),
                pltpu.VMEM((2, CHIPS, NCLASS, ROWS, NY), F32),
                pltpu.VMEM((CHIPS, NCLASS, ROWS, NY), F32),
                pltpu.VMEM((CHIPS, NCLASS, ROWS, NY), F32),
                pltpu.VMEM((CHIPS, NCLASS, ROWS, NY), F32),
                pltpu.VMEM((NCLASS, ROWS, NY), F32),
                pltpu.SemaphoreType.REGULAR,
                dma((5,)),
                dma,
                dma((2, CHUNKS)),
                dma((2, CHUNKS)),
                dma((2,)),
                dma((2,)),
                dma((3, GROUP)),
                dma((3, GROUP)),
                dma((2, CHIPS)),
                dma((2, CHIPS)),
                dma((2, CHIPS)),
                dma((2, CHIPS)),
            ],
            compiler_params=pltpu.CompilerParams(
                collective_id=0, has_side_effects=True, vmem_limit_bytes=63 << 20
            ),
        )(tracers, courant_x, courant_y, kdiff, humidity, land, band_class, opt_table, hyg_table)
    )


def solution(mesh):
    in_specs = (
        P("tracer", None, "tile", None),
        P("tracer", "tile", None),
        P("tracer", "tile", None),
        P("tracer", "tile", None),
        P("tracer", "tile", None),
        P("tile", None),
        P(),
        P(),
        P(),
    )
    out_specs = (P("tracer", None, "tile", None), P("tracer", None, "tile", None))
    return jax.shard_map(
        functools.partial(local, mesh.shape["tile"]),
        mesh=mesh, in_specs=in_specs, out_specs=out_specs, check_vma=False,
    )
```

```python
import functools

import jax
import jax.numpy as jnp
from jax import lax
from jax.experimental import pallas as pl
from jax.experimental.pallas import tpu as pltpu
from jax.sharding import PartitionSpec as P

MESH = pl.DeviceIdType.MESH
F32 = jnp.float32
TR = 12
LEV = 8
ROWS = 8
NY = 128
NCLASS = 8
BANDS = 14
GROUP = 8
CHIPS = 4
PER = 6
CHUNKS = TR // PER

V, V2, XJ0, XJ1, XS0, XS1, XS2, GA, GB, HA, HB, YJ0, YJ1, YS0, YS1, YS2, INV, UP, LOW = range(19)
NCOEF = 19
ROWS_CHUNK = PER * LEV * ROWS


def limited(near, far):
    return jnp.minimum(jnp.maximum(near, jnp.minimum(far, 0.0)), jnp.maximum(far, 0.0))


def roll_rows(a, by):
    return pltpu.roll(a, by % ROWS, 0)


def roll_lanes(a, by):
    return pltpu.roll(a, by % NY, 1)


def face_coefs(c):
    plus, minus = jnp.maximum(c, 0.0), jnp.minimum(c, 0.0)
    return plus, plus * (0.5 * (1.0 - c)), minus, minus * (-0.5 * (1.0 + c))


def kernel(
    tiles,
    x_hbm, cx_hbm, cy_hbm, kd_hbm, hum_hbm, land_hbm, cls_ref, opt_ref, hyg_ref,
    out_ref, ext_ref,
    ext, fields, kd, hum, land, coef, shift, jumps, middle_ref, sbuf, spair, sx, sr, swell,
    ready, loc, own, hs, hr, es, er, gs, gr, ps, pr, xs, xr,
):
    me, k = lax.axis_index("tile"), lax.axis_index("tracer")
    right, left = lax.rem(me + 1, tiles), lax.rem(me + tiles - 1, tiles)
    chip, core = k // 2, lax.rem(k, 2)

    loads = [
        pltpu.make_async_copy(cx_hbm, fields.at[pl.ds(k, 1), 0, pl.ds(4, ROWS)], loc.at[0]),
        pltpu.make_async_copy(cy_hbm, fields.at[pl.ds(k, 1), 1, pl.ds(4, ROWS)], loc.at[1]),
        pltpu.make_async_copy(kd_hbm, kd, loc.at[2]),
        pltpu.make_async_copy(hum_hbm, hum, loc.at[3]),
        pltpu.make_async_copy(land_hbm, land, loc.at[4]),
    ]
    for copy in loads:
        copy.start()

    barrier = pltpu.get_barrier_semaphore()
    pl.semaphore_signal(barrier, inc=1, device_id=(left, k), device_id_type=MESH)
    for step in range(1, GROUP):
        pl.semaphore_signal(
            barrier, inc=1, device_id=(me, lax.rem(k + step, GROUP)), device_id_type=MESH
        )
    own_copy = pltpu.make_async_copy(x_hbm, ext.at[:, :, pl.ds(4, ROWS), :], own)
    own_copy.start()
    pl.semaphore_wait(barrier, GROUP)
    pl.semaphore_signal(ready, inc=1, device_id=(right, k), device_id_type=MESH)

    def halo(half, chunk):
        t = pl.ds(chunk * PER, PER)
        return pltpu.make_async_remote_copy(
            src_ref=x_hbm.at[t, :, pl.ds(4 - 4 * half, 4), :],
            dst_ref=ext.at[t, :, pl.ds(12 * half, 4), :],
            send_sem=hs.at[half, chunk],
            recv_sem=hr.at[half, chunk],
            device_id=((left if half else right), k),
            device_id_type=MESH,
        )

    def edge(half):
        src, dst, count = ((10, 2, 2), (4, 12, 4))[half]
        return pltpu.make_async_remote_copy(
            src_ref=fields.at[k, :, pl.ds(src, count), :],
            dst_ref=fields.at[k, :, pl.ds(dst, count), :],
            send_sem=es.at[half],
            recv_sem=er.at[half],
            device_id=((left if half else right), k),
            device_id_type=MESH,
        )

    def spread(part, step):
        first, count = ((2, 2), (12, 4), (4, ROWS))[part]
        return pltpu.make_async_remote_copy(
            src_ref=fields.at[k, :, pl.ds(first, count), :],
            dst_ref=fields.at[k, :, pl.ds(first, count), :],
            send_sem=gs.at[part, step],
            recv_sem=gr.at[part, k],
            device_id=(me, lax.rem(k + step, GROUP)),
            device_id_type=MESH,
        )

    def spread_wait(part, step):
        first, count = ((2, 2), (12, 4), (4, ROWS))[part]
        other = lax.rem(k + step, GROUP)
        pltpu.make_async_remote_copy(
            src_ref=fields.at[other, :, pl.ds(first, count), :],
            dst_ref=fields.at[other, :, pl.ds(first, count), :],
            send_sem=gs.at[part, step],
            recv_sem=gr.at[part, other],
            device_id=(me, other),
            device_id_type=MESH,
        ).wait_recv()

    halo(0, 0).start()
    for copy in loads:
        copy.wait()
    lowest = jnp.where(k == LEV - 1, 1.0, 0.0).astype(F32)
    fields[k, 2, pl.ds(4, ROWS), :] = kd[0] * (
        1.0 + lowest * (0.25 + 0.75 * land[...].astype(F32) - 1.0)
    )
    edge(0).start()
    for step in range(1, GROUP):
        spread(2, step).start()
    for chunk in range(1, CHUNKS):
        halo(0, chunk).start()

    dryness = jnp.log(1.0 - hum[0])
    for c in range(NCLASS):
        swell[c] = jnp.exp(-hyg_ref[c] * dryness)

    pl.semaphore_wait(ready, 1)
    edge(1).start()
    for chunk in range(CHUNKS):
        halo(1, chunk).start()

    for half in (1, 0):
        edge(half).wait_recv()
        for step in range(1, GROUP):
            spread(half, step).start()
    for part in (2, 1, 0):
        for step in range(1, GROUP):
            spread_wait(part, step)

    from_y = lax.broadcasted_iota(jnp.int32, (2 * NY, NY), 0) % NY
    to_y = lax.broadcasted_iota(jnp.int32, (2 * NY, NY), 1)
    for n in range(4):
        plus = jnp.where(from_y == (to_y + n + NY - 1) % NY, 1.0, 0.0)
        minus = jnp.where(from_y == (to_y + n + NY - 2) % NY, 1.0, 0.0)
        shift[:, pl.ds(n * NY, NY)] = (plus - minus).astype(jnp.bfloat16)
    sbuf[...] = jnp.zeros_like(sbuf)

    def coefficients(half):
        base = 4 * half
        upper = previous = None
        for level in range(LEV):
            c0 = fields[level, 0, pl.ds(base + 2, ROWS), :]
            c1 = fields[level, 0, pl.ds(base + 3, ROWS), :]
            p0, r0, q0, t0 = face_coefs(c0)
            p1, r1, q1, t1 = face_coefs(c1)
            put = lambda row, value: coef.__setitem__((half, level, row), value)
            put(XJ0, -p0)
            put(XJ1, -q1)
            put(XS0, r0)
            put(XS1, t0 - r1)
            put(XS2, -t1)
            put(GA, p1)
            put(GB, r1)
            put(HA, q0)
            put(HB, t0)
            d0 = fields[level, 1, pl.ds(base + 2, ROWS), :]
            d1 = roll_lanes(d0, -1)
            put(V, 1.0 + (c0 - c1) + (d0 - d1))
            put(V2, 1.0 + (d0 - d1))
            p0, r0, q0, t0 = face_coefs(d0)
            p1, r1, q1, t1 = face_coefs(d1)
            put(YJ0, -p0)
            put(YJ1, -q1)
            put(YS0, r0)
            put(YS1, t0 - r1)
            put(YS2, -t1)
            lower = fields[level, 2, pl.ds(base + 2, ROWS), :]
            if level == 0:
                inverse = 1.0 / (1.0 + lower)
                put(UP, jnp.zeros_like(inverse))
            else:
                inverse = 1.0 / (1.0 + upper + lower - upper * previous)
                put(UP, upper * inverse)
            previous = lower * inverse
            upper = lower
            put(INV, inverse)
            put(LOW, previous)

    coefficients(1)
    coefficients(0)
    own_copy.wait()

    def mixed(moved, half):
        forward = []
        for level in range(LEV):
            solved = moved[level] * coef[half, level, INV]
            if level:
                solved = solved + coef[half, level, UP] * forward[-1]
            forward.append(solved)
        for level in range(LEV - 2, -1, -1):
            forward[level] = forward[level] + coef[half, level, LOW] * forward[level + 1]
        return forward

    def jumps_along_y(v):
        lead = v.astype(jnp.bfloat16)
        trail = (v - lead.astype(F32)).astype(jnp.bfloat16)
        jumps[...] = jnp.dot(
            jnp.concatenate([lead, trail], 1), shift[...], preferred_element_type=F32
        )

    def along_y(row, c):
        jump = [jumps[pl.ds(row, ROWS), pl.ds(n * NY, NY)] for n in range(4)]
        slope = [limited(jump[n], jump[n + 1]) for n in range(3)]
        return (
            (c(YJ0) * jump[1] + c(YJ1) * jump[2])
            + (c(YS0) * slope[0] + c(YS1) * slope[1])
            + c(YS2) * slope[2]
        )

    def first_step(i, t, half):
        base = 4 * half
        moved = []
        for level in range(LEV):
            c = lambda row: coef[half, level, row]
            v = [ext[t, level, pl.ds(base + n, ROWS), :] for n in range(5)]
            jump = [v[n + 1] - v[n] for n in range(4)]
            slope = [limited(jump[n], jump[n + 1]) for n in range(3)]
            row = pl.multiple_of((i * LEV + level) * ROWS, ROWS)
            moved.append(
                (c(V) * v[2] + c(XJ0) * jump[1])
                + (c(XJ1) * jump[2] + c(XS0) * slope[0])
                + (c(XS1) * slope[1] + c(XS2) * slope[2])
                + along_y(row, c)
            )
        moved = mixed(moved, half)
        for level in range(LEV):
            row = pl.multiple_of((i * LEV + level) * ROWS, ROWS)
            middle_ref[pl.ds(row, ROWS), :] = moved[level]

    def second_step(i, t, half):
        moved = []
        for level in range(LEV):
            c = lambda row: coef[half, level, row]
            row = pl.multiple_of((i * LEV + level) * ROWS, ROWS)
            m = middle_ref[pl.ds(row, ROWS), :]
            jump = m - roll_rows(m, 1)
            slope = limited(jump, roll_rows(jump, -1))
            flux = roll_rows(c(GA) * m + c(GB) * slope, 1) + c(HA) * m + c(HB) * slope
            moved.append((c(V2) * m + flux) - roll_rows(flux, -1) + along_y(row, c))
        final = mixed(moved, half)
        for level in range(LEV):
            out_ref[t, level, pl.ds(4 * half, 4), :] = final[level][2:6, :]

    def do_chunk(half, chunk):
        halo(half, chunk).wait_recv()
        first = chunk * PER
        own_rows = ext[pl.ds(first, PER), :, pl.ds(4 * half + 2, ROWS), :]
        jumps_along_y(own_rows.reshape(ROWS_CHUNK, NY))

        def first_body(i, carry):
            first_step(i, first + i, half)
            return carry

        def second_body(i, carry):
            second_step(i, first + i, half)
            return carry

        lax.fori_loop(0, PER, first_body, 0)
        jumps_along_y(middle_ref[...])
        lax.fori_loop(0, PER, second_body, 0)
        rows = pl.ds(4 * half, 4)
        weights = []
        for i in range(PER):
            own_class = cls_ref[k * TR + first + i]
            weights.append([jnp.where(own_class == c, 1.0, 0.0).astype(F32) for c in range(NCLASS)])
        for level in range(LEV):
            values = [out_ref[first + i, level, rows, :] for i in range(PER)]
            at = (level % 2, level // 2)
            for c in range(NCLASS):
                total = sum(weights[i][c] * values[i] for i in range(PER))
                sbuf[at[0], at[1], c, rows, :] = sbuf[at[0], at[1], c, rows, :] + total

    def pair(half, step):
        to = lax.rem(chip + step, CHIPS)
        rows = pl.ds(4 * half, 4)
        return pltpu.make_async_remote_copy(
            src_ref=sbuf.at[1 - core, to, :, rows, :],
            dst_ref=spair.at[to, :, rows, :],
            send_sem=ps.at[half, step],
            recv_sem=pr.at[half, step],
            device_id=(me, 2 * chip + 1 - core),
            device_id_type=MESH,
        )

    def cross(half, step):
        to = lax.rem(chip + step, CHIPS)
        rows = pl.ds(4 * half, 4)
        return pltpu.make_async_remote_copy(
            src_ref=sx.at[to, :, rows, :],
            dst_ref=sr.at[step, :, rows, :],
            send_sem=xs.at[half, step],
            recv_sem=xr.at[half, step],
            device_id=(me, 2 * to + core),
            device_id_type=MESH,
        )

    def start_pair(half):
        for step in (2, 1, 3, 0):
            pair(half, step).start()

    def start_cross(half):
        rows = pl.ds(4 * half, 4)
        for step in (2, 1, 3, 0):
            pair(half, step).wait_recv()
            to = lax.rem(chip + step, CHIPS)
            sx[to, :, rows, :] = sbuf[core, to, :, rows, :] + spair[to, :, rows, :]
            if step:
                cross(half, step).start()

    def after_body(chunk, carry):
        do_chunk(1, chunk)
        return carry

    def before_body(chunk, carry):
        do_chunk(0, chunk)

        @pl.when(chunk == 0)
        def _():
            start_cross(1)

        return carry

    lax.fori_loop(0, CHUNKS, after_body, 0)
    start_pair(1)
    lax.fori_loop(0, CHUNKS, before_body, 0)
    start_pair(0)
    start_cross(0)
    for half in (1, 0):
        for step in range(1, CHIPS):
            cross(half, step).wait_recv()
    wetted = []
    for c in range(NCLASS):
        total = (sx[chip, c] + sr[1, c]) + (sr[2, c] + sr[3, c])
        wetted.append(total * swell[c])
    for b in range(BANDS):
        ext_ref[0, b] = sum(opt_ref[c, b] * wetted[c] for c in range(NCLASS))

    for half in (0, 1):
        edge(half).wait_send()
        for chunk in range(CHUNKS):
            halo(half, chunk).wait_send()
        for step in range(CHIPS):
            pair(half, step).wait_send()
            if step:
                cross(half, step).wait_send()
    for part in range(3):
        for step in range(1, GROUP):
            spread(part, step).wait_send()


def local(tiles, tracers, courant_x, courant_y, kdiff, humidity, land, band_class, opt_table, hyg_table):
    hbm = pl.BlockSpec(memory_space=pltpu.HBM)
    vmem = pl.BlockSpec(memory_space=pltpu.VMEM)
    smem = pl.BlockSpec(memory_space=pltpu.SMEM)
    dma = pltpu.SemaphoreType.DMA
    return tuple(
        pl.pallas_call(
            functools.partial(kernel, tiles),
            out_shape=(
                jax.ShapeDtypeStruct((TR, LEV, ROWS, NY), F32),
                jax.ShapeDtypeStruct((1, BANDS, ROWS, NY), F32),
            ),
            in_specs=[hbm] * 6 + [smem] * 3,
            out_specs=(vmem, vmem),
            scratch_shapes=[
                pltpu.VMEM((TR, LEV, 16, NY), F32),
                pltpu.VMEM((LEV, 3, 16, NY), F32),
                pltpu.VMEM((1, ROWS, NY), F32),
                pltpu.VMEM((1, ROWS, NY), F32),
                pltpu.VMEM((ROWS, NY), jnp.int32),
                pltpu.VMEM((2, LEV, NCOEF, ROWS, NY), F32),
                pltpu.VMEM((2 * NY, 4 * NY), jnp.bfloat16),
                pltpu.VMEM((ROWS_CHUNK, 4 * NY), F32),
                pltpu.VMEM((ROWS_CHUNK, NY), F32),
                pltpu.VMEM((2, CHIPS, NCLASS, ROWS, NY), F32),
                pltpu.VMEM((CHIPS, NCLASS, ROWS, NY), F32),
                pltpu.VMEM((CHIPS, NCLASS, ROWS, NY), F32),
                pltpu.VMEM((CHIPS, NCLASS, ROWS, NY), F32),
                pltpu.VMEM((NCLASS, ROWS, NY), F32),
                pltpu.SemaphoreType.REGULAR,
                dma((5,)),
                dma,
                dma((2, CHUNKS)),
                dma((2, CHUNKS)),
                dma((2,)),
                dma((2,)),
                dma((3, GROUP)),
                dma((3, GROUP)),
                dma((2, CHIPS)),
                dma((2, CHIPS)),
                dma((2, CHIPS)),
                dma((2, CHIPS)),
            ],
            compiler_params=pltpu.CompilerParams(
                collective_id=0, has_side_effects=True, vmem_limit_bytes=63 << 20
            ),
        )(tracers, courant_x, courant_y, kdiff, humidity, land, band_class, opt_table, hyg_table)
    )


def solution(mesh):
    in_specs = (
        P("tracer", None, "tile", None),
        P("tracer", "tile", None),
        P("tracer", "tile", None),
        P("tracer", "tile", None),
        P("tracer", "tile", None),
        P("tile", None),
        P(),
        P(),
        P(),
    )
    out_specs = (P("tracer", None, "tile", None), P("tracer", None, "tile", None))
    return jax.shard_map(
        functools.partial(local, mesh.shape["tile"]),
        mesh=mesh, in_specs=in_specs, out_specs=out_specs, check_vma=False,
    )
```
